768 devices in a mesh: dp: 48 (over z, y_lo), tensor: 16 (over x, y_hi, core).
Axes of the slice: x: 4, y: 8 (y_hi: 2, y_lo: 4; y = y_hi * 4 + y_lo), z: 12, core: 2. Of those that a mesh axis runs over, the one named last changes fastest.
Arguments:
- resid: bfloat16 [6144, 8192], P('dp', 'tensor'), may hold values from -6 to 6
- attn_out: bfloat16 [6144, 8192], P('dp', 'tensor'), may hold values from -6 to 6
- w_out: bfloat16 [8192, 8192], P('tensor'), may hold values from -0.0625 to 0.0625
- proj: bfloat16 [3072, 8192], P(None, 'tensor'), may hold values from -0.109375 to 0.109375
- student_in: bfloat16 [11520, 3072], P(('dp', 'tensor')), may hold values from -24 to 24
- dest: int32 [6144, 1], replicated, may hold values from 0 to 47; in each aligned block of 128 rows (0 to 127, 128 to 255, ...) at most 5 rows name the same one
Outputs:
- grad_proj: float32 [3072, 8192], P('dp', 'tensor')
The draws below stay inside these ranges and needn't reach their ends.
Inputs may be any that keep to these rules, and one draw needn't show every extreme that they name: `dest`: within each aligned block of 128 rows (one teacher group) no student group is named by more than 5 rows, a bound that some block reaches.
All inputs are finite; a program needn't handle non-finite values.
Results may differ from the reference program's by a relative error of at most 0.0095.
Values may be sent and summed in bfloat16 or wider, within the bound.
No kernel may reach another device: no remote copies, remote signals or barrier semaphores. Data moves between devices by JAX's collectives and lax.ppermute only.
A program may use at most 64 MiB of HBM per device.

```python
import math
import jax
import jax.numpy as jnp
import numpy as np
from jax import lax

D = 8192
DS = 3072
ROWS = 128
CAP = 5
SLOTS = 240
TOKENS = 6144
N_DP = 48
N_TENSOR = 16


def with_spikes(result, own_key, source, target, blocks, factor):
    def block_of(dim):
        return (jnp.arange(result.shape[dim]) // (result.shape[dim] // blocks)).reshape((-1,) + (1,) * (result.ndim - 1 - dim))

    near = jax.random.permutation(own_key, blocks)[block_of(target)]
    other_side = (block_of(target) + blocks // 2) % blocks
    return jnp.where((block_of(source) == near) | (block_of(source) == other_side), factor * result, result)


def steps_of(own_key, shape, cuts, smallest, largest):
    factor_of, own = 1.0, jax.random.fold_in(own_key, 6)
    for dim, parts in cuts:
        heights = jnp.exp(jax.random.uniform(jax.random.fold_in(own, dim), (parts,), jnp.float32, smallest / len(cuts), largest / len(cuts)))
        factor_of = factor_of * jnp.repeat(heights, shape[dim] // parts).reshape([-1 if axis == dim else 1 for axis in range(len(shape))])
    return factor_of


def shared_out(own_key, own, number, rows, count, top, most, skew):
    sequence = jax.random.permutation(own_key, count)
    heavy_load, common = shares(count, rows * top, most, skew, True), shares(count, rows * top, most, skew, False)
    places = jnp.arange(count)

    def named(tallies, offset_by):
        used = int((tallies > 0).sum())
        fixed = max(1, used // 4)
        shifted = fixed + (places - fixed + offset_by * (used - fixed)) % max(1, count - fixed)
        return jnp.zeros((count,), jnp.int32).at[sequence[jnp.where(places < fixed, places, shifted)]].set(jnp.asarray(tallies, jnp.int32))

    tallies = jnp.where(number % 4 == 0, named(heavy_load, number // 4), named(common, number - number // 4 - 1))
    mixed = jax.random.permutation(jax.random.fold_in(own, 3), count)
    giver, taker = mixed[0:count // 2 * 2:2], mixed[1:count // 2 * 2:2]
    room = jnp.minimum(tallies[giver] - 1, most - tallies[taker]) // 2
    room = jnp.where((giver == sequence[0]) | (taker == sequence[0]) | (tallies[taker] == 0), 0, jnp.maximum(room, 0))
    shifted = jax.random.randint(jax.random.fold_in(own, 4), (count // 2,), 0, 1 << 20) % (room + 1)
    tallies = tallies.at[giver].add(-shifted).at[taker].add(shifted)
    members = jnp.searchsorted(jnp.cumsum(tallies), jnp.arange(rows * top), side="right").astype(jnp.int32)
    grid = members.reshape(top, rows).T
    grid = grid[jax.random.permutation(jax.random.fold_in(own, 1), rows)]
    offset_by = jax.random.randint(jax.random.fold_in(own, 2), (rows, 1), 0, top)
    return jnp.take_along_axis(grid, (jnp.arange(top)[None, :] + offset_by) % top, axis=1)


def shares(amount, total, limit, slope, full):
    portions = [(1 << 20) // math.isqrt(grade ** slope) + 1 for grade in range(1, amount + 1)]
    largest = limit if full else min(limit, max(-(-total // amount), total * portions[0] // sum(portions)))
    least = 1 if total - largest >= amount - 1 else 0
    holding, rest = [largest] + [least] * (amount - 1), total - largest - least * (amount - 1)
    while rest > 0:
        candidates = [i for i in range(1, amount) if holding[i] < largest] or [i for i in range(1, amount) if holding[i] < limit]
        mass, budget = sum([portions[i] for i in candidates]), rest
        for i in candidates:
            extra = min(limit - holding[i], max(1, budget * portions[i] // mass), rest)
            holding[i] = holding[i] + extra
            rest = rest - extra
    return np.array(holding)


def noise(stream_key, dims, width, reach, pieces=(), held_as=jnp.bfloat16):
    drawn = jax.random.normal(stream_key, dims, jnp.float32) * width
    if len(pieces) > 0:
        drawn = steps_of(stream_key, dims, pieces, -0.22, 0.18) * drawn
    return jnp.clip(drawn, min=-reach, max=reach).astype(held_as)


def heavy_noise(rng, shape, deviation, bound, pieces, heavy, kind=jnp.bfloat16):
    result = deviation * jax.random.normal(rng, shape, jnp.float32)
    if pieces:
        result = result * steps_of(rng, shape, pieces, -0.22, 0.18)
    return jnp.clip(with_spikes(result, jax.random.fold_in(rng, 3), *heavy), -bound, bound).astype(kind)


def setup_inputs(seed: int = 0) -> dict:
    keys = jax.random.split(jax.random.key(seed), 7)
    resid = noise(keys[0], (TOKENS, D), 1.0, 6.0, ((0, 48), (1, 16)))
    attn_out = noise(keys[1], (TOKENS, D), 1.0, 6.0, ((0, 48), (1, 16)))
    w_out = noise(keys[2], (D, D), D ** -0.5, 0.0625, ((0, 16),))
    proj = noise(keys[3], (DS, D), DS ** -0.5, 0.109375, ((1, 16),))
    student_in = heavy_noise(keys[4], (N_DP * SLOTS, DS), 1.0, 24.0, ((0, 768),), (0, 1, 768, 6.0))
    dest_keys = jax.random.split(jax.random.fold_in(keys[5], 1), TOKENS // ROWS)
    dest_turns = jax.random.permutation(jax.random.fold_in(keys[5], 3), TOKENS // ROWS)
    dest = jax.vmap(lambda own, number: shared_out(jax.random.fold_in(keys[5], 2), own, number, ROWS, N_DP, 1, CAP, 2))(dest_keys, dest_turns).reshape((TOKENS, 1))
    return {"resid": resid, "attn_out": attn_out, "w_out": w_out, "proj": proj, "student_in": student_in, "dest": dest}


def reference(resid, attn_out, w_out, proj, student_in, dest):
    block_width = D // N_TENSOR

    def add_block(running, block_index):
        first_col = block_index * block_width
        head_cols = lax.dynamic_slice_in_dim(attn_out, first_col, block_width, 1)
        weight_rows = lax.dynamic_slice_in_dim(w_out, first_col, block_width, 0)
        head_term = jnp.dot(head_cols, weight_rows, preferred_element_type=jnp.float32).astype(jnp.bfloat16)
        head_term = lax.optimization_barrier(head_term)
        return running + head_term.astype(jnp.float32), None

    summed = lax.scan(add_block, jnp.zeros((TOKENS, D), jnp.float32), jnp.arange(N_TENSOR, dtype=jnp.int32))[0]
    hidden = (resid.astype(jnp.float32) + summed).astype(jnp.bfloat16)
    dest_table = dest[:, 0].reshape(N_DP, ROWS)
    group_iota = jnp.arange(N_DP, dtype=jnp.int32)
    onehot = (dest_table[:, :, None] == group_iota[None, None, :]).astype(jnp.int32)
    slot_rank = jnp.sum((jnp.cumsum(onehot, axis=1) - 1) * onehot, axis=2)
    slot_index = dest_table * CAP + slot_rank
    slot_iota = jnp.arange(N_DP * CAP, dtype=jnp.int32)

    def pack_rows(packing_args):
        src_slots, src_rows = packing_args
        selector = (src_slots[None, :] == slot_iota[:, None]).astype(jnp.bfloat16)
        return jnp.dot(selector, src_rows, preferred_element_type=jnp.float32).astype(jnp.bfloat16)

    packed = lax.map(pack_rows, (slot_index, hidden.reshape(N_DP, ROWS, D)))
    targets = packed.reshape(N_DP, N_DP, CAP, D).transpose(1, 0, 2, 3).reshape(N_DP * SLOTS, D)
    counts = jnp.sum(onehot, axis=1)
    valid_slot = (jnp.arange(CAP, dtype=jnp.int32)[None, None, :] < counts.T[:, :, None]).reshape(N_DP * SLOTS)
    predicted = jnp.dot(student_in, proj, preferred_element_type=jnp.float32)
    mismatch = (jnp.where(valid_slot[:, None], predicted - targets.astype(jnp.float32), 0.0) / ROWS).astype(jnp.bfloat16)
    return lax.dot_general(student_in, mismatch, (((0,), (0,)), ((), ())), preferred_element_type=jnp.float32)
```

```python
import jax
import jax.numpy as jnp
from jax import lax
from jax.sharding import Mesh, PartitionSpec as P

bf16 = jnp.bfloat16
f32 = jnp.float32
AXES = ("z", "yl", "x", "yh", "core")
DP = ("z", "yl")
TENSOR = ("x", "yh", "core")
PAD = 8


def swap(value, axis):
    return lax.ppermute(value, axis, [(0, 1), (1, 0)])


def pick(value, index, axis=0):
    return lax.dynamic_index_in_dim(value, index, axis, keepdims=False)


def gather_pair(value, axis):
    other = swap(value, axis)
    me = lax.axis_index(axis)
    first = jnp.where(me == 0, value, other)
    second = jnp.where(me == 0, other, value)
    return jnp.stack([first, second])


def gather_tensor(value):
    value = gather_pair(value, "yh")
    value = lax.all_gather(value, "x", axis=0, tiled=False)
    value = gather_pair(value, "core")
    return jnp.moveaxis(value, 0, 2)


def local(resid, attn_out, w_out, proj, student_in, dest):
    n_z, n_yl = lax.axis_size("z"), lax.axis_size("yl")
    n_x, n_yh, n_c = lax.axis_size("x"), lax.axis_size("yh"), lax.axis_size("core")
    groups = n_z * n_yl
    n_t = n_x * n_yh * n_c
    my_group = lax.axis_index(DP)
    my_yl, my_yh, my_core = lax.axis_index("yl"), lax.axis_index("yh"), lax.axis_index("core")
    rows, width = attn_out.shape
    own, ds = student_in.shape
    cap = own * n_t // groups
    per = groups // n_t

    padded = jnp.pad(student_in, ((0, 1), (0, 0)))
    slots = own + 1
    whole = gather_tensor(padded).reshape(n_t * slots, ds)
    quarters = padded.reshape(slots, n_z, n_yl, ds // groups).transpose(2, 0, 1, 3)
    quarters = quarters.reshape(n_yl, slots, ds // n_yl)
    quarter = lax.all_to_all(quarters, "yl", 0, 0, tiled=True)
    quarter = gather_tensor(quarter).reshape(n_t * n_yl * slots, ds // n_yl)

    partial = jnp.dot(attn_out, w_out, preferred_element_type=f32).astype(bf16)
    partial = partial.reshape(rows, n_x, n_yh, n_c, width)
    given = pick(partial, 1 - my_core, 3)
    kept = pick(partial, my_core, 3)
    summed = kept.astype(f32) + swap(given, "core").astype(f32)
    summed = summed.astype(bf16).transpose(1, 2, 0, 3)
    summed = lax.all_to_all(summed, "x", 0, 0, tiled=True)
    summed = jnp.sum(summed.astype(f32), axis=0)
    given = pick(summed, 1 - my_yh).astype(bf16)
    kept = pick(summed, my_yh)
    hidden = (resid.astype(f32) + kept + swap(given, "yh").astype(f32)).astype(bf16)

    dest_table = dest[:, 0].reshape(groups, rows)
    own_dest = pick(dest_table, my_group)
    row_iota = jnp.arange(rows, dtype=jnp.int32)
    same = (own_dest[:, None] == own_dest[None, :]) & (row_iota[None, :] < row_iota[:, None])
    slot_rank = jnp.sum(same.astype(jnp.int32), axis=1)
    slot_index = own_dest * PAD + slot_rank
    selector = (
        slot_index[None, :] == jnp.arange(groups * PAD, dtype=jnp.int32)[:, None]
    ).astype(bf16)
    packed = jnp.dot(selector, hidden, preferred_element_type=f32).astype(bf16)
    arrived = lax.all_to_all(
        packed.reshape(groups, PAD, width), DP, 0, 0, tiled=True
    ).reshape(groups * PAD, width)
    slot = jnp.arange(n_t * slots, dtype=jnp.int32)
    part, place = slot // slots, slot % slots
    origin = jnp.where(place < own, (part * per + place // cap) * PAD + place % cap, -1)
    placing = (origin[:, None] == jnp.arange(groups * PAD, dtype=jnp.int32)[None, :]).astype(bf16)
    targets = jnp.dot(placing, arrived, preferred_element_type=f32)
    counts = jnp.sum((dest_table == my_group).astype(jnp.int32), axis=1)
    filled = (jnp.arange(PAD, dtype=jnp.int32)[None, :] < counts[:, None]).reshape(groups * PAD)
    valid = jnp.dot(placing, filled.astype(bf16)[:, None], preferred_element_type=f32) > 0.5

    predicted = jnp.dot(whole, proj, preferred_element_type=f32)
    mismatch = (jnp.where(valid, predicted - targets, 0.0) / rows).astype(bf16)

    mismatch = lax.all_gather(mismatch.reshape(n_t, slots, width), "yl", axis=1)
    mismatch = mismatch.reshape(n_t * n_yl * slots, width)
    partial_grad = lax.dot_general(
        quarter, mismatch, (((0,), (0,)), ((), ())), preferred_element_type=f32
    ).astype(bf16)
    partial_grad = lax.all_to_all(
        partial_grad.reshape(n_z, ds // groups, width), "z", 0, 0, tiled=True
    )
    return jnp.sum(partial_grad.astype(f32), axis=0)


def solution(mesh):
    fine = Mesh(mesh.devices.reshape(12, 4, 4, 2, 2), AXES)
    return jax.shard_map(
        local,
        mesh=fine,
        in_specs=(
            P(DP, TENSOR),
            P(DP, TENSOR),
            P(TENSOR, None),
            P(None, TENSOR),
            P(DP + TENSOR, None),
            P(),
        ),
        out_specs=P(DP, TENSOR),
        check_vma=False,
    )
```

```python
import jax
import jax.numpy as jnp
from jax import lax
from jax.experimental import pallas as pl
from jax.experimental.pallas import tpu as pltpu
from jax.sharding import Mesh, PartitionSpec as P

bf16 = jnp.bfloat16
f32 = jnp.float32
AXES = ("z", "yl", "x", "yh", "core")
DP = ("z", "yl")
TENSOR = ("x", "yh", "core")
PAD = 8


def meet(value, axis, bit):
    return lax.ppermute(value, axis, [(i, i ^ bit) for i in range(lax.axis_size(axis))])


def joined(value, axis, bit):
    return jnp.concatenate([value, meet(value, axis, bit)], axis=0)


def shift(value, axis, step):
    size = lax.axis_size(axis)
    return lax.ppermute(value, axis, [(i, (i + step) % size) for i in range(size)])


def pick(value, index, axis=0):
    return lax.dynamic_index_in_dim(value, index, axis, keepdims=False)


def after(value, other):
    return lax.optimization_barrier((value, other))[0]


def product_kernel(core_ref, rows_ref, weight_ref, *refs):
    *added, out_ref, held, arrived = refs
    blocks, _, width = held.shape
    copies = []
    for k in range(blocks):
        first = pl.multiple_of((2 * k + core_ref[0]) * width, width)
        copies.append(
            pltpu.make_async_copy(weight_ref.at[:, pl.ds(first, width)], held.at[k], arrived.at[k])
        )
    for copy in copies:
        copy.start()
    for k, copy in enumerate(copies):
        copy.wait()
        block = jnp.dot(rows_ref[...], held[k], preferred_element_type=f32)
        for ref in added:
            block = block + ref[k].astype(f32)
        out_ref[k] = block.astype(bf16)


def half_product(rows, weight, core, blocks, *added):
    n, depth = rows.shape
    width = weight.shape[1] // (2 * blocks)
    return pl.pallas_call(
        product_kernel,
        in_specs=[
            pl.BlockSpec(memory_space=pltpu.SMEM),
            pl.BlockSpec(memory_space=pltpu.VMEM),
            pl.BlockSpec(memory_space=pltpu.HBM),
        ]
        + [pl.BlockSpec(memory_space=pltpu.VMEM) for _ in added],
        out_specs=pl.BlockSpec(memory_space=pltpu.VMEM),
        out_shape=jax.ShapeDtypeStruct((blocks, n, width), bf16),
        scratch_shapes=[
            pltpu.VMEM((blocks, depth, width), bf16),
            pltpu.SemaphoreType.DMA((blocks,)),
        ],
        cost_estimate=pl.CostEstimate(
            flops=2 * n * depth * width * blocks,
            bytes_accessed=2 * blocks * width * (depth + n),
            transcendentals=0,
        ),
        compiler_params=pltpu.CompilerParams(vmem_limit_bytes=52 * 1024 * 1024),
    )(core.reshape(1), rows, weight, *added)


def local(resid, attn_out, w_out, proj, student_in, dest):
    n_z, n_yl = lax.axis_size("z"), lax.axis_size("yl")
    n_x, n_yh, n_c = lax.axis_size("x"), lax.axis_size("yh"), lax.axis_size("core")
    groups = n_z * n_yl
    n_t = n_x * n_yh * n_c
    my_group = lax.axis_index(DP)
    my_yl, my_x = lax.axis_index("yl"), lax.axis_index("x")
    my_yh, my_core = lax.axis_index("yh"), lax.axis_index("core")
    rows, width = attn_out.shape
    own, ds = student_in.shape
    cap = own * n_t // groups
    per = groups // n_t
    slots = own + 1
    part = ds // n_yl

    given = half_product(attn_out, w_out, 1 - my_core, n_x * n_yh)
    taken = meet(given, "core", 1)

    whole = jnp.pad(student_in, ((0, 1), (0, 0)))
    whole = whole.reshape(slots, n_z, n_yl, ds // groups).transpose(0, 2, 1, 3).reshape(slots, ds)
    whole = joined(whole, "yh", 1)

    slot = jnp.arange(n_t * slots, dtype=jnp.int32)
    place, order = slot % slots, slot // slots
    from_yh = my_yh ^ (order % n_yh)
    from_x = my_x ^ (order // n_yh % n_x)
    from_core = my_core ^ (order // (n_yh * n_x))
    holder = (from_x * n_yh + from_yh) * n_c + from_core
    origin = jnp.where(place < own, (holder * per + place // cap) * PAD + place % cap, -1)
    placing = (origin[:, None] == jnp.arange(groups * PAD, dtype=jnp.int32)[None, :]).astype(bf16)
    dest_table = dest[:, 0].reshape(groups, rows)
    counts = jnp.sum((dest_table == my_group).astype(jnp.int32), axis=1)
    filled = (jnp.arange(PAD, dtype=jnp.int32)[None, :] < counts[:, None]).reshape(groups * PAD)
    valid = jnp.dot(placing, filled.astype(bf16)[:, None], preferred_element_type=f32) > 0.5
    own_dest = pick(dest_table, my_group)
    row_iota = jnp.arange(rows, dtype=jnp.int32)
    same = (own_dest[:, None] == own_dest[None, :]) & (row_iota[None, :] < row_iota[:, None])
    slot_rank = jnp.sum(same.astype(jnp.int32), axis=1)
    slot_index = own_dest * PAD + slot_rank
    selector = (
        slot_index[None, :] == jnp.arange(groups * PAD, dtype=jnp.int32)[:, None]
    ).astype(bf16)

    summed = half_product(attn_out, w_out, my_core, n_x * n_yh, taken)
    summed, whole = lax.optimization_barrier((summed, whole))
    whole = joined(whole, "x", 1)

    def lanes(k):
        first = lax.rem(my_yl + k, n_yl) * part
        return lax.dynamic_slice_in_dim(whole, first, part, 1)

    quarter = [lanes(0)] + [shift(lanes(k), "yl", k) for k in range(1, n_yl)]
    weight = after(proj, whole).reshape(n_z, n_yl, ds // groups, width).transpose(1, 0, 2, 3)
    summed = summed.reshape(n_x, n_yh * rows, width)
    summed = lax.all_to_all(summed, "x", 0, 0, tiled=True)
    summed = jnp.sum(summed.astype(f32), axis=0).reshape(n_yh, rows, width)
    given = pick(summed, 1 - my_yh).astype(bf16)
    kept = resid.astype(f32) + pick(summed, my_yh)
    given, whole = lax.optimization_barrier((given, whole))
    taken = meet(given, "yh", 1)
    whole = joined(whole, "x", 2)
    taken, whole = lax.optimization_barrier((taken, whole))
    hidden = (kept + taken.astype(f32)).astype(bf16)

    packed = jnp.dot(selector, hidden, preferred_element_type=f32).astype(bf16)
    quarter = joined(after(jnp.concatenate(quarter, axis=1), packed), "x", 2)
    whole = joined(after(whole, packed), "core", 1)
    predicted = jnp.dot(whole, weight.reshape(ds, width), preferred_element_type=f32)
    arrived = lax.all_to_all(
        packed.reshape(groups, PAD, width), DP, 0, 0, tiled=True
    ).reshape(groups * PAD, width)
    targets = jnp.dot(placing, arrived, preferred_element_type=f32)
    mismatch = (jnp.where(valid, predicted - targets, 0.0) / rows).astype(bf16)

    quarter = joined(after(quarter, arrived), "core", 1)
    mismatches = [mismatch] + [shift(mismatch, "yl", k) for k in range(1, n_yl)]
    partial_grad = sum(
        lax.dot_general(
            quarter[:, k * part : (k + 1) * part],
            mismatches[k],
            (((0,), (0,)), ((), ())),
            preferred_element_type=f32,
        )
        for k in range(n_yl)
    )
    partial_grad = lax.all_to_all(
        partial_grad.astype(bf16).reshape(n_z, ds // groups, width), "z", 0, 0, tiled=True
    )
    return jnp.sum(partial_grad.astype(f32), axis=0)


def solution(mesh):
    fine = Mesh(mesh.devices.reshape(12, 4, 4, 2, 2), AXES)
    return jax.shard_map(
        local,
        mesh=fine,
        in_specs=(
            P(DP, TENSOR),
            P(DP, TENSOR),
            P(TENSOR, None),
            P(None, TENSOR),
            P(DP + TENSOR, None),
            P(),
        ),
        out_specs=P(DP, TENSOR),
        check_vma=False,
    )
```

```python
import jax
import jax.numpy as jnp
from jax import lax
from jax.experimental import pallas as pl
from jax.experimental.pallas import tpu as pltpu
from jax.sharding import Mesh, PartitionSpec as P

bf16 = jnp.bfloat16
f32 = jnp.float32
AXES = ("z", "yl", "x", "yh", "core")
DP = ("z", "yl")
TENSOR = ("x", "yh", "core")
PAD = 8


def meet(value, axis, bit):
    return lax.ppermute(value, axis, [(i, i ^ bit) for i in range(lax.axis_size(axis))])


def joined(value, axis, bit):
    return jnp.concatenate([value, meet(value, axis, bit)], axis=1)


def shift(value, axis, step):
    size = lax.axis_size(axis)
    return lax.ppermute(value, axis, [(i, (i + step) % size) for i in range(size)])


def pick(value, index, axis=0):
    return lax.dynamic_index_in_dim(value, index, axis, keepdims=False)


def after(value, other):
    return lax.optimization_barrier((value, other))[0]


def product_kernel(core_ref, rows_ref, weight_ref, *refs):
    *added, out_ref, held, arrived = refs
    blocks, _, width = held.shape
    copies = []
    for k in range(blocks):
        first = pl.multiple_of((2 * k + core_ref[0]) * width, width)
        copies.append(
            pltpu.make_async_copy(weight_ref.at[:, pl.ds(first, width)], held.at[k], arrived.at[k])
        )
    for copy in copies:
        copy.start()
    for k, copy in enumerate(copies):
        copy.wait()
        block = jnp.dot(rows_ref[...], held[k], preferred_element_type=f32)
        for ref in added:
            block = block + ref[k].astype(f32)
        out_ref[k] = block.astype(bf16)


def half_product(rows, weight, core, blocks, *added):
    n, depth = rows.shape
    width = weight.shape[1] // (2 * blocks)
    return pl.pallas_call(
        product_kernel,
        in_specs=[
            pl.BlockSpec(memory_space=pltpu.SMEM),
            pl.BlockSpec(memory_space=pltpu.VMEM),
            pl.BlockSpec(memory_space=pltpu.HBM),
        ]
        + [pl.BlockSpec(memory_space=pltpu.VMEM) for _ in added],
        out_specs=pl.BlockSpec(memory_space=pltpu.VMEM),
        out_shape=jax.ShapeDtypeStruct((blocks, n, width), bf16),
        scratch_shapes=[
            pltpu.VMEM((blocks, depth, width), bf16),
            pltpu.SemaphoreType.DMA((blocks,)),
        ],
        cost_estimate=pl.CostEstimate(
            flops=2 * n * depth * width * blocks,
            bytes_accessed=2 * blocks * width * (depth + n),
            transcendentals=0,
        ),
        compiler_params=pltpu.CompilerParams(vmem_limit_bytes=52 * 1024 * 1024),
    )(core.reshape(1), rows, weight, *added)


def local(resid, attn_out, w_out, proj, student_in, dest):
    n_z, n_yl = lax.axis_size("z"), lax.axis_size("yl")
    n_x, n_yh, n_c = lax.axis_size("x"), lax.axis_size("yh"), lax.axis_size("core")
    groups = n_z * n_yl
    n_t = n_x * n_yh * n_c
    my_group = lax.axis_index(DP)
    my_x, my_yh, my_core = (lax.axis_index(axis) for axis in TENSOR)
    rows, width = attn_out.shape
    own, ds = student_in.shape
    cap = own * n_t // groups
    per = groups // n_t
    slots = own + 1
    part = ds // n_yl

    given = half_product(attn_out, w_out, 1 - my_core, n_x * n_yh)
    taken = meet(given, "core", 1)

    block = jnp.pad(student_in, ((0, 1), (0, 0)))
    block = block.reshape(slots, n_z, n_yl, ds // groups).transpose(2, 0, 1, 3)
    block = block.reshape(n_yl, slots, part)
    block = jnp.concatenate([block, lax.all_to_all(block, "yl", 0, 0, tiled=True)], axis=0)
    block = joined(block, "yh", 1)

    slot = jnp.arange(n_t * own, dtype=jnp.int32)
    place, order = slot % own, slot // own
    from_yh = my_yh ^ (order % n_yh)
    from_x = (my_x + n_x - order // n_yh % n_x) % n_x
    from_core = my_core ^ (order // (n_yh * n_x))
    holder = (from_x * n_yh + from_yh) * n_c + from_core
    origin = (holder * per + place // cap) * PAD + place % cap
    placing = (origin[:, None] == jnp.arange(groups * PAD, dtype=jnp.int32)[None, :]).astype(bf16)
    kept_rows = order * slots + place
    closing = (kept_rows[:, None] == jnp.arange(n_t * slots, dtype=jnp.int32)[None, :]).astype(bf16)
    dest_table = dest[:, 0].reshape(groups, rows)
    counts = jnp.sum((dest_table == my_group).astype(jnp.int32), axis=1)
    filled = (jnp.arange(PAD, dtype=jnp.int32)[None, :] < counts[:, None]).reshape(groups * PAD)
    valid = jnp.dot(placing, filled.astype(bf16)[:, None], preferred_element_type=f32) > 0.5
    own_dest = pick(dest_table, my_group)
    row_iota = jnp.arange(rows, dtype=jnp.int32)
    same = (own_dest[:, None] == own_dest[None, :]) & (row_iota[None, :] < row_iota[:, None])
    slot_rank = jnp.sum(same.astype(jnp.int32), axis=1)
    slot_index = own_dest * PAD + slot_rank
    selector = (
        slot_index[None, :] == jnp.arange(groups * PAD, dtype=jnp.int32)[:, None]
    ).astype(bf16)

    summed = half_product(attn_out, w_out, my_core, n_x * n_yh, taken)
    block = after(block, summed)
    block = jnp.concatenate([block] + [shift(block, "x", k) for k in range(1, n_x)], axis=1)
    weight = proj.reshape(n_z, n_yl, ds // groups, width).transpose(1, 0, 2, 3)
    weight = weight.reshape(n_yl, part, width)
    summed = summed.reshape(n_x, n_yh * rows, width)
    summed = lax.all_to_all(summed, "x", 0, 0, tiled=True)
    summed = jnp.sum(summed.astype(f32), axis=0).reshape(n_yh, rows, width)
    given = pick(summed, 1 - my_yh).astype(bf16)
    kept = resid.astype(f32) + pick(summed, my_yh)
    taken = meet(given, "yh", 1)
    taken, block, weight = lax.optimization_barrier((taken, block, weight))
    hidden = (kept + taken.astype(f32)).astype(bf16)

    packed = jnp.dot(selector, hidden, preferred_element_type=f32).astype(bf16)
    block = joined(after(block, packed), "core", 1)
    parts = lax.optimization_barrier(
        [jnp.dot(closing, rows16, preferred_element_type=f32).astype(bf16) for rows16 in block]
    )
    predicted = sum(
        jnp.dot(parts[k], weight[k], preferred_element_type=f32) for k in range(n_yl)
    )
    arrived = lax.all_to_all(
        packed.reshape(groups, PAD, width), DP, 0, 0, tiled=True
    ).reshape(groups * PAD, width)
    targets = jnp.dot(placing, arrived, preferred_element_type=f32)
    mismatch = (jnp.where(valid, predicted - targets, 0.0) / rows).astype(bf16)

    mismatch = lax.all_gather(mismatch, "yl", axis=0, tiled=True)
    mismatch = mismatch.reshape(n_yl, n_t * own, width)
    partial_grad = sum(
        lax.dot_general(
            parts[n_yl + k], mismatch[k], (((0,), (0,)), ((), ())), preferred_element_type=f32
        )
        for k in range(n_yl)
    )
    partial_grad = lax.all_to_all(
        partial_grad.astype(bf16).reshape(n_z, ds // groups, width), "z", 0, 0, tiled=True
    )
    return jnp.sum(partial_grad.astype(f32), axis=0)


def solution(mesh):
    fine = Mesh(mesh.devices.reshape(12, 4, 4, 2, 2), AXES)
    return jax.shard_map(
        local,
        mesh=fine,
        in_specs=(
            P(DP, TENSOR),
            P(DP, TENSOR),
            P(TENSOR, None),
            P(None, TENSOR),
            P(DP + TENSOR, None),
            P(),
        ),
        out_specs=P(DP, TENSOR),
        check_vma=False,
    )
```

```python
import jax
import jax.numpy as jnp
from jax import lax
from jax.experimental import pallas as pl
from jax.experimental.pallas import tpu as pltpu
from jax.sharding import Mesh, PartitionSpec as P

bf16 = jnp.bfloat16
f32 = jnp.float32
AXES = ("z", "yl", "x", "yh", "core")
DP = ("z", "yl")
TENSOR = ("x", "yh", "core")
PAD = 8


def meet(value, axis, bit):
    return lax.ppermute(value, axis, [(i, i ^ bit) for i in range(lax.axis_size(axis))])


def joined(value, axis, bit):
    return jnp.concatenate([value, meet(value, axis, bit)], axis=1)


def shift(value, axis, step):
    size = lax.axis_size(axis)
    return lax.ppermute(value, axis, [(i, (i + step) % size) for i in range(size)])


def pick(value, index, axis=0):
    return lax.dynamic_index_in_dim(value, index, axis, keepdims=False)


def after(value, other):
    return lax.optimization_barrier((value, other))[0]


def product_kernel(core_ref, rows_ref, weight_ref, *refs):
    *added, out_ref, held, arrived = refs
    blocks, _, width = held.shape
    copies = []
    for k in range(blocks):
        first = pl.multiple_of((2 * k + core_ref[0]) * width, width)
        copies.append(
            pltpu.make_async_copy(weight_ref.at[:, pl.ds(first, width)], held.at[k], arrived.at[k])
        )
    for copy in copies:
        copy.start()
    for k, copy in enumerate(copies):
        copy.wait()
        block = jnp.dot(rows_ref[...], held[k], preferred_element_type=f32)
        for ref in added:
            block = block + ref[k].astype(f32)
        out_ref[k] = block.astype(bf16)


def half_product(rows, weight, core, blocks, *added):
    n, depth = rows.shape
    width = weight.shape[1] // (2 * blocks)
    return pl.pallas_call(
        product_kernel,
        in_specs=[
            pl.BlockSpec(memory_space=pltpu.SMEM),
            pl.BlockSpec(memory_space=pltpu.VMEM),
            pl.BlockSpec(memory_space=pltpu.HBM),
        ]
        + [pl.BlockSpec(memory_space=pltpu.VMEM) for _ in added],
        out_specs=pl.BlockSpec(memory_space=pltpu.VMEM),
        out_shape=jax.ShapeDtypeStruct((blocks, n, width), bf16),
        scratch_shapes=[
            pltpu.VMEM((blocks, depth, width), bf16),
            pltpu.SemaphoreType.DMA((blocks,)),
        ],
        cost_estimate=pl.CostEstimate(
            flops=2 * n * depth * width * blocks,
            bytes_accessed=2 * blocks * width * (depth + n),
            transcendentals=0,
        ),
        compiler_params=pltpu.CompilerParams(vmem_limit_bytes=52 * 1024 * 1024),
    )(core.reshape(1), rows, weight, *added)


def local(resid, attn_out, w_out, proj, student_in, dest):
    n_z, n_yl = lax.axis_size("z"), lax.axis_size("yl")
    n_x, n_yh, n_c = lax.axis_size("x"), lax.axis_size("yh"), lax.axis_size("core")
    groups = n_z * n_yl
    n_t = n_x * n_yh * n_c
    my_group = lax.axis_index(DP)
    my_x, my_yh, my_core = (lax.axis_index(axis) for axis in TENSOR)
    rows, width = attn_out.shape
    own, ds = student_in.shape
    cap = own * n_t // groups
    per = groups // n_t
    slots = own + 1
    part = ds // n_yl

    given = half_product(attn_out, w_out, 1 - my_core, n_x * n_yh)
    taken = meet(given, "core", 1)

    block = jnp.pad(student_in, ((0, 1), (0, 0)))
    block = block.reshape(slots, n_z, n_yl, ds // groups).transpose(2, 0, 1, 3)
    block = block.reshape(n_yl, slots, part)
    block = jnp.concatenate([block, lax.all_to_all(block, "yl", 0, 0, tiled=True)], axis=0)
    block = joined(block, "yh", 1)

    slot = jnp.arange(n_t * own, dtype=jnp.int32)
    place, order = slot % own, slot // own
    from_yh = my_yh ^ (order % n_yh)
    from_x = (my_x + n_x - order // n_yh % n_x) % n_x
    from_core = my_core ^ (order // (n_yh * n_x))
    holder = (from_x * n_yh + from_yh) * n_c + from_core
    origin = (holder * per + place // cap) * PAD + place % cap
    placing = (origin[:, None] == jnp.arange(groups * PAD, dtype=jnp.int32)[None, :]).astype(bf16)
    kept_rows = order * slots + place
    closing = (kept_rows[:, None] == jnp.arange(n_t * slots, dtype=jnp.int32)[None, :]).astype(bf16)
    dest_table = dest[:, 0].reshape(groups, rows)
    counts = jnp.sum((dest_table == my_group).astype(jnp.int32), axis=1)
    filled = (jnp.arange(PAD, dtype=jnp.int32)[None, :] < counts[:, None]).reshape(groups * PAD)
    valid = jnp.dot(placing, filled.astype(bf16)[:, None], preferred_element_type=f32) > 0.5
    own_dest = pick(dest_table, my_group)
    row_iota = jnp.arange(rows, dtype=jnp.int32)
    same = (own_dest[:, None] == own_dest[None, :]) & (row_iota[None, :] < row_iota[:, None])
    slot_rank = jnp.sum(same.astype(jnp.int32), axis=1)
    slot_index = own_dest * PAD + slot_rank
    selector = (
        slot_index[None, :] == jnp.arange(groups * PAD, dtype=jnp.int32)[:, None]
    ).astype(bf16)

    summed = half_product(attn_out, w_out, my_core, n_x * n_yh, taken)
    block = after(block, summed)
    block = jnp.concatenate([block] + [shift(block, "x", k) for k in range(1, n_x)], axis=1)
    summed = summed.reshape(n_x, n_yh * rows, width)
    summed = lax.all_to_all(summed, "x", 0, 0, tiled=True)
    summed = jnp.sum(summed.astype(f32), axis=0).reshape(n_yh, rows, width)
    given = pick(summed, 1 - my_yh).astype(bf16)
    kept = resid.astype(f32) + pick(summed, my_yh)
    taken = meet(given, "yh", 1)
    hidden = (kept + taken.astype(f32)).astype(bf16)

    packed = jnp.dot(selector, hidden, preferred_element_type=f32).astype(bf16)
    block = joined(after(block, packed), "core", 1)
    weight = after(proj, packed).reshape(n_z, n_yl, ds // groups, width).transpose(1, 0, 2, 3)
    weight = weight.reshape(n_yl, part, width)
    parts = lax.optimization_barrier(
        [jnp.dot(closing, rows16, preferred_element_type=f32).astype(bf16) for rows16 in block]
    )
    predicted = sum(
        jnp.dot(parts[k], weight[k], preferred_element_type=f32) for k in range(n_yl)
    )
    arrived = lax.all_to_all(
        packed.reshape(groups, PAD, width), DP, 0, 0, tiled=True
    ).reshape(groups * PAD, width)
    targets = jnp.dot(placing, arrived, preferred_element_type=f32)
    mismatch = (jnp.where(valid, predicted - targets, 0.0) / rows).astype(bf16)

    mismatch = lax.all_gather(mismatch, "yl", axis=0, tiled=True)
    mismatch = mismatch.reshape(n_yl, n_t * own, width)
    partial_grad = sum(
        lax.dot_general(
            parts[n_yl + k], mismatch[k], (((0,), (0,)), ((), ())), preferred_element_type=f32
        )
        for k in range(n_yl)
    )
    partial_grad = lax.all_to_all(
        partial_grad.astype(bf16).reshape(n_z, ds // groups, width), "z", 0, 0, tiled=True
    )
    return jnp.sum(partial_grad.astype(f32), axis=0)


def solution(mesh):
    fine = Mesh(mesh.devices.reshape(12, 4, 4, 2, 2), AXES)
    return jax.shard_map(
        local,
        mesh=fine,
        in_specs=(
            P(DP, TENSOR),
            P(DP, TENSOR),
            P(TENSOR, None),
            P(None, TENSOR),
            P(DP + TENSOR, None),
            P(),
        ),
        out_specs=P(DP, TENSOR),
        check_vma=False,
    )
```

```python
import jax
import jax.numpy as jnp
from jax import lax
from jax.experimental import pallas as pl
from jax.experimental.pallas import tpu as pltpu
from jax.sharding import Mesh, PartitionSpec as P

bf16 = jnp.bfloat16
f32 = jnp.float32
AXES = ("z", "yl", "x", "yh", "core")
DP = ("z", "yl")
TENSOR = ("x", "yh", "core")
PAD = 8


def meet(value, axis, bit):
    return lax.ppermute(value, axis, [(i, i ^ bit) for i in range(lax.axis_size(axis))])


def joined(value, axis, bit):
    return jnp.concatenate([value, meet(value, axis, bit)], axis=1)


def shift(value, axis, step):
    size = lax.axis_size(axis)
    return lax.ppermute(value, axis, [(i, (i + step) % size) for i in range(size)])


def pick(value, index, axis=0):
    return lax.dynamic_index_in_dim(value, index, axis, keepdims=False)


def after(value, other):
    return lax.optimization_barrier((value, other))[0]


def product_kernel(core_ref, rows_ref, weight_ref, *refs):
    *added, out_ref, rows_held, held, added_held, rows_sem, sems, added_sems = refs
    blocks, _, width = held.shape
    rows_copy = pltpu.make_async_copy(rows_ref, rows_held, rows_sem)
    copies = []
    for k in range(blocks):
        first = pl.multiple_of((2 * k + core_ref[0]) * width, width)
        pair = [pltpu.make_async_copy(weight_ref.at[:, pl.ds(first, width)], held.at[k], sems.at[k])]
        for ref in added:
            pair.append(pltpu.make_async_copy(ref.at[k], added_held.at[k], added_sems.at[k]))
        copies.append(pair)
    rows_copy.start()
    for pair in copies:
        for copy in pair:
            copy.start()
    rows_copy.wait()
    for k, pair in enumerate(copies):
        for copy in pair:
            copy.wait()
        block = jnp.dot(rows_held[...], held[k], preferred_element_type=f32)
        if added:
            block = block + added_held[k].astype(f32)
        out_ref[k] = block.astype(bf16)


def half_product(rows, weight, core, blocks, *added):
    n, depth = rows.shape
    width = weight.shape[1] // (2 * blocks)
    return pl.pallas_call(
        product_kernel,
        in_specs=[
            pl.BlockSpec(memory_space=pltpu.SMEM),
            pl.BlockSpec(memory_space=pltpu.HBM),
            pl.BlockSpec(memory_space=pltpu.HBM),
        ]
        + [pl.BlockSpec(memory_space=pltpu.HBM) for _ in added],
        out_specs=pl.BlockSpec(memory_space=pltpu.VMEM),
        out_shape=jax.ShapeDtypeStruct((blocks, n, width), bf16),
        scratch_shapes=[
            pltpu.VMEM((n, depth), bf16),
            pltpu.VMEM((blocks, depth, width), bf16),
            pltpu.VMEM((blocks, n, width), bf16),
            pltpu.SemaphoreType.DMA,
            pltpu.SemaphoreType.DMA((blocks,)),
            pltpu.SemaphoreType.DMA((blocks,)),
        ],
        cost_estimate=pl.CostEstimate(
            flops=2 * n * depth * width * blocks,
            bytes_accessed=2 * blocks * width * (depth + n),
            transcendentals=0,
        ),
        compiler_params=pltpu.CompilerParams(vmem_limit_bytes=52 * 1024 * 1024),
    )(core.reshape(1), rows, weight, *added)


def local(resid, attn_out, w_out, proj, student_in, dest):
    n_z, n_yl = lax.axis_size("z"), lax.axis_size("yl")
    n_x, n_yh, n_c = lax.axis_size("x"), lax.axis_size("yh"), lax.axis_size("core")
    groups = n_z * n_yl
    n_t = n_x * n_yh * n_c
    my_group = lax.axis_index(DP)
    my_x, my_yh, my_core = (lax.axis_index(axis) for axis in TENSOR)
    rows, width = attn_out.shape
    own, ds = student_in.shape
    cap = own * n_t // groups
    per = groups // n_t
    slots = own + 1
    part = ds // n_yl

    given = half_product(attn_out, w_out, 1 - my_core, n_x * n_yh)
    taken = meet(given, "core", 1)

    block = jnp.pad(student_in, ((0, 1), (0, 0)))
    block = block.reshape(slots, n_z, n_yl, ds // groups).transpose(2, 0, 1, 3)
    block = block.reshape(n_yl, slots, part)
    block = jnp.concatenate([block, lax.all_to_all(block, "yl", 0, 0, tiled=True)], axis=0)
    block = joined(block, "yh", 1)

    slot = jnp.arange(n_t * own, dtype=jnp.int32)
    place, order = slot % own, slot // own
    from_yh = my_yh ^ (order % n_yh)
    from_x = (my_x + n_x - order // n_yh % n_x) % n_x
    from_core = my_core ^ (order // (n_yh * n_x))
    holder = (from_x * n_yh + from_yh) * n_c + from_core
    origin = (holder * per + place // cap) * PAD + place % cap
    placing = (origin[:, None] == jnp.arange(groups * PAD, dtype=jnp.int32)[None, :]).astype(bf16)
    kept_rows = order * slots + place
    closing = (kept_rows[:, None] == jnp.arange(n_t * slots, dtype=jnp.int32)[None, :]).astype(bf16)
    dest_table = dest[:, 0].reshape(groups, rows)
    counts = jnp.sum((dest_table == my_group).astype(jnp.int32), axis=1)
    filled = (jnp.arange(PAD, dtype=jnp.int32)[None, :] < counts[:, None]).reshape(groups * PAD)
    valid = jnp.dot(placing, filled.astype(bf16)[:, None], preferred_element_type=f32) > 0.5
    own_dest = pick(dest_table, my_group)
    row_iota = jnp.arange(rows, dtype=jnp.int32)
    same = (own_dest[:, None] == own_dest[None, :]) & (row_iota[None, :] < row_iota[:, None])
    slot_rank = jnp.sum(same.astype(jnp.int32), axis=1)
    slot_index = own_dest * PAD + slot_rank
    selector = (
        slot_index[None, :] == jnp.arange(groups * PAD, dtype=jnp.int32)[:, None]
    ).astype(bf16)

    summed = half_product(attn_out, w_out, my_core, n_x * n_yh, taken)
    summed = summed.reshape(n_x, n_yh * rows, width)
    summed = lax.all_to_all(summed, "x", 0, 0, tiled=True)
    summed = jnp.sum(summed.astype(f32), axis=0).reshape(n_yh, rows, width)
    given = pick(summed, 1 - my_yh).astype(bf16)
    kept = resid.astype(f32) + pick(summed, my_yh)
    taken = meet(given, "yh", 1)
    block = after(block, given)
    block = jnp.concatenate([block] + [shift(block, "x", k) for k in range(1, n_x)], axis=1)
    hidden = (kept + taken.astype(f32)).astype(bf16)

    packed = jnp.dot(selector, hidden, preferred_element_type=f32).astype(bf16)
    block = joined(after(block, packed), "core", 1)
    weight = after(proj, packed).reshape(n_z, n_yl, ds // groups, width).transpose(1, 0, 2, 3)
    weight = weight.reshape(n_yl, part, width)
    parts = lax.optimization_barrier(
        [jnp.dot(closing, rows16, preferred_element_type=f32).astype(bf16) for rows16 in block]
    )
    predicted = sum(
        jnp.dot(parts[k], weight[k], preferred_element_type=f32) for k in range(n_yl)
    )
    arrived = lax.all_to_all(
        packed.reshape(groups, PAD, width), DP, 0, 0, tiled=True
    ).reshape(groups * PAD, width)
    targets = jnp.dot(placing, arrived, preferred_element_type=f32)
    mismatch = (jnp.where(valid, predicted - targets, 0.0) / rows).astype(bf16)

    mismatch = lax.all_gather(mismatch, "yl", axis=0, tiled=True)
    mismatch = mismatch.reshape(n_yl, n_t * own, width)
    partial_grad = sum(
        lax.dot_general(
            parts[n_yl + k], mismatch[k], (((0,), (0,)), ((), ())), preferred_element_type=f32
        )
        for k in range(n_yl)
    )
    partial_grad = lax.all_to_all(
        partial_grad.astype(bf16).reshape(n_z, ds // groups, width), "z", 0, 0, tiled=True
    )
    return jnp.sum(partial_grad.astype(f32), axis=0)


def solution(mesh):
    fine = Mesh(mesh.devices.reshape(12, 4, 4, 2, 2), AXES)
    return jax.shard_map(
        local,
        mesh=fine,
        in_specs=(
            P(DP, TENSOR),
            P(DP, TENSOR),
            P(TENSOR, None),
            P(None, TENSOR),
            P(DP + TENSOR, None),
            P(),
        ),
        out_specs=P(DP, TENSOR),
        check_vma=False,
    )
```
